32 devices in a mesh: tm: 4 (over y, x), inp: 8 (over z, core).
Axes of the slice: x: 2, y: 2, z: 4, core: 2. Of those that a mesh axis runs over, the one named last changes fastest.
Arguments:
- voltages: bfloat16 [1024, 524288], P('inp', 'tm'), may hold values from -6 to 6
- coefficients: float32 [16, 8192], replicated, may hold values from -1.5 to 1.5
Outputs:
- visibilities: float32 [2, 128, 1024, 1024], P(None, ('tm', 'inp'))
The draws below stay inside these ranges and needn't reach their ends.
All inputs are finite; a program needn't handle non-finite values.
Results may differ from the reference program's by a relative error of at most 0.0003.
Values may be sent and summed in bfloat16 or wider, within the bound.
A program may use at most 192 MiB of HBM per device.

```python
import math
import jax
import jax.numpy as jnp
from jax import lax

NFFT = 8192
TAPS = 16
INPUTS = 1024
CH = 128
CH0 = 1024
SPECTRA = 64
SAMPLES = 524288


def block_levels(key, shape, shards, smallest, largest):
    loudness, own = 1.0, jax.random.fold_in(key, 6)
    for position, parts in shards:
        steps = jnp.exp(jax.random.uniform(jax.random.fold_in(own, position), (parts,), jnp.float32, smallest / len(shards), largest / len(shards)))
        loudness = loudness * jnp.repeat(steps, shape[position] // parts).reshape([-1 if axis == position else 1 for axis in range(len(shape))])
    return loudness


def gaussian(rng, extent, width, bound, pieces=(), kind=jnp.bfloat16):
    level = block_levels(rng, extent, pieces, -0.22, 0.18) if pieces else 1.0
    array = jax.random.normal(rng, extent, jnp.float32) * width * level
    return jnp.minimum(jnp.maximum(array, -bound), bound).astype(kind)


def setup_inputs(seed: int = 0) -> dict:
    seeds = jax.random.split(jax.random.key(seed), 3)
    return {
        "voltages": gaussian(seeds[0], (INPUTS, SAMPLES), 1.0, 6.0, ((0, 8), (1, 4))),
        "coefficients": gaussian(seeds[1], (TAPS, NFFT), 0.25, 1.5, (), jnp.float32),
    }


def channelize(row, coefficients):
    signal = row.astype(jnp.float32)
    padded = jnp.concatenate([jnp.zeros((TAPS - 1, NFFT), jnp.float32), signal], axis=0)
    filtered = jnp.zeros((SPECTRA, NFFT), jnp.float32)
    for tap in range(TAPS):
        filtered = filtered + coefficients[tap] * padded[TAPS - 1 - tap:TAPS - 1 - tap + SPECTRA]
    spectrum = jnp.fft.rfft(filtered, axis=-1)[:, CH0:CH0 + CH] * (NFFT ** -0.5)
    return jnp.stack([jnp.real(spectrum), jnp.imag(spectrum)]).astype(filtered.dtype)


def correlate(pair):
    real_part, imag_part = pair[0], pair[1]
    vis_real = jnp.dot(real_part.T, real_part, precision=lax.Precision.HIGHEST) + jnp.dot(imag_part.T, imag_part, precision=lax.Precision.HIGHEST)
    cross = jnp.dot(imag_part.T, real_part, precision=lax.Precision.HIGHEST)
    vis_imag = cross - cross.T
    return jnp.stack([vis_real, vis_imag]) / SPECTRA


def reference(voltages, coefficients):
    frames = voltages.reshape(INPUTS, SPECTRA, NFFT)
    group = math.gcd(INPUTS, 16)
    grouped = frames.reshape(INPUTS // group, group, SPECTRA, NFFT)
    spectra = lax.map(lambda block: jax.vmap(lambda row: channelize(row, coefficients))(block), grouped)
    spectra = spectra.reshape(INPUTS, 2, SPECTRA, CH).transpose(3, 1, 2, 0)
    result = lax.map(correlate, spectra)
    return result.transpose(1, 0, 2, 3)
```

```python
import math

import jax
import jax.numpy as jnp
from jax import lax
from jax.sharding import PartitionSpec as P

NFFT = 8192
TAPS = 16
CH = 128
CH0 = 1024


def shifted(shard, axis, by):
    count = lax.axis_size(axis)
    pairs = [(i, i + by) for i in range(count) if 0 <= i + by < count]
    return lax.ppermute(shard, axis, pairs)


def dft_table():
    samples = jnp.arange(NFFT, dtype=jnp.int32)
    channel = CH0 + jnp.arange(CH, dtype=jnp.int32)
    phase = samples[:, None] * channel[None, :] % NFFT
    angle = phase.astype(jnp.float32) * (2.0 * math.pi / NFFT)
    return jnp.concatenate([jnp.cos(angle), -jnp.sin(angle)], axis=1) * NFFT ** (-0.5)


def filter_frames(history, frames, coefficients):
    count = frames.shape[1]
    padded = jnp.concatenate([history, frames], axis=1)
    filtered = coefficients[0] * padded[:, TAPS - 1 : TAPS - 1 + count].astype(jnp.float32)
    for tap in range(1, TAPS):
        window = padded[:, TAPS - 1 - tap : TAPS - 1 - tap + count].astype(jnp.float32)
        filtered = filtered + coefficients[tap] * window
    return filtered


def transform(filtered, table):
    rows = filtered.reshape(-1, NFFT)
    return jnp.dot(rows, table, precision=lax.Precision.HIGH, preferred_element_type=jnp.float32)


def shards(voltages, coefficients):
    inp_count = voltages.shape[0]
    frames = voltages.reshape(inp_count, -1, NFFT)
    s_count = frames.shape[1]
    table = dft_table()
    blank = jnp.zeros((inp_count, TAPS - 1, NFFT), jnp.bfloat16)
    filtered = filter_frames(blank, frames, coefficients)
    spectra = transform(filtered, table).reshape(inp_count, s_count, 2 * CH)
    last_frames = frames[:, s_count - (TAPS - 1) :]
    carried = filter_frames(last_frames, blank, coefficients)
    carried_spec = transform(carried, table).reshape(inp_count, TAPS - 1, 2 * CH)
    arrived = shifted(carried_spec, "tm", 1)
    spectra = jnp.concatenate([spectra[:, : TAPS - 1] + arrived, spectra[:, TAPS - 1 :]], axis=1)
    outgoing = spectra.reshape(inp_count, s_count, 2, CH).transpose(2, 3, 1, 0)
    outgoing = outgoing.reshape(2, CH, 1, 1, s_count * inp_count)
    n_time = lax.axis_size("tm")
    n_input = lax.axis_size("inp")
    received = lax.all_to_all(outgoing, ("tm", "inp"), split_axis=1, concat_axis=2, tiled=True)
    received = received.reshape(2, -1, n_time, n_input, s_count * inp_count)
    owned = received.shape[1]
    gathered = received.reshape(2, owned, n_time, n_input, s_count, inp_count)
    gathered = gathered.transpose(0, 1, 2, 4, 3, 5).reshape(
        2, owned, n_time * s_count, n_input * inp_count
    )
    real_part, imag_part = gathered[0], gathered[1]
    left = jnp.stack(
        [
            jnp.concatenate([real_part, imag_part], axis=1),
            jnp.concatenate([imag_part, real_part], axis=1),
        ]
    )
    right = jnp.stack(
        [
            jnp.concatenate([real_part, imag_part], axis=1),
            jnp.concatenate([real_part, -imag_part], axis=1),
        ]
    ) / (n_time * s_count)
    return jnp.einsum(
        "pcsa,pcsb->pcab",
        left,
        right,
        precision=lax.Precision.HIGH,
        preferred_element_type=jnp.float32,
    )


def solution(mesh):
    in_specs = (P("inp", "tm"), P())
    out_specs = P(None, ("tm", "inp"), None, None)
    return jax.shard_map(shards, mesh=mesh, in_specs=in_specs, out_specs=out_specs, check_vma=False)
```
